128 devices in a mesh: dp: 8 (over y, core), tensor: 16 (over z, x).
Axes of the slice: x: 4, y: 4, z: 4, core: 2. Of those that a mesh axis runs over, the one named last changes fastest.
Arguments:
- hidden: bfloat16 [1024, 53248], P('dp', 'tensor'), may hold values from -6 to 6
- exponents: int32 [1024], P('dp'), may hold values from -3 to 0
- weight_levels: bfloat16 [53248, 16384], P('tensor', 'dp'), may hold values from -8 to 7
- column_scale: float32 [16384], P('dp'), may hold values from 0.00043335953 to 0.0043335953
- residual: bfloat16 [1024, 16384], P('tensor', 'dp'), may hold values from -6 to 6
Outputs:
- layer_output: bfloat16 [1024, 16384], P('tensor', 'dp')
The draws below stay inside these ranges and needn't reach their ends.
All inputs are finite; a program needn't handle non-finite values.
Results may differ from the reference program's by a relative error of at most 0.018.
Values may be sent and summed in bfloat16 or wider, within the bound.
A program may use at most 128 MiB of HBM per device.

```python
import math
import jax
import jax.numpy as jnp
import numpy as np
from jax import lax

D = 16384
FF = 53248
HAD_SMALL = 52
ROWS = 1024


def draw_weight_levels(key, part):
    key = jax.random.fold_in(key, 7)
    levels = jax.random.randint(key, (FF, D), -8, 8, dtype=jnp.int32)
    return levels.astype(jnp.float32).astype(jnp.bfloat16)


def place_ends(drawn, stream_key, smallest, largest):
    index_at = [jax.random.randint(jax.random.fold_in(stream_key, axis), (), 0, length) for axis, length in enumerate(drawn.shape)]
    longest = drawn.shape.index(max(drawn.shape))
    next_to = index_at[:longest] + [(index_at[longest] + 1) % drawn.shape[longest]] + index_at[longest + 1:]
    return drawn.at[tuple(index_at)].set(smallest).at[tuple(next_to)].set(largest)


def steps_of(own_key, extent, split, low, largest):
    level, own = 1.0, jax.random.fold_in(own_key, 6)
    for axis_at, parts in split:
        steps = jnp.exp(jax.random.uniform(jax.random.fold_in(own, axis_at), (parts,), jnp.float32, low / len(split), largest / len(split)))
        level = level * jnp.repeat(steps, extent[axis_at] // parts).reshape([-1 if axis == axis_at else 1 for axis in range(len(extent))])
    return level


def gaussian(rng, shape, spread, limit, cuts=(), kind=jnp.bfloat16):
    drawn = jax.random.normal(rng, shape, jnp.float32) * spread
    if len(cuts) > 0:
        drawn = steps_of(rng, shape, cuts, -0.22, 0.18) * drawn
    return jnp.clip(drawn, min=-limit, max=limit).astype(kind)


def setup_inputs(seed: int = 0) -> dict:
    streams_of = jax.random.split(jax.random.key(seed), 6)
    hidden = gaussian(streams_of[0], (ROWS, FF), 1.0, 6.0, ((0, 8), (1, 16)))
    exponents = place_ends(jax.random.randint(streams_of[1], (ROWS,), -3, 1), jax.random.fold_in(streams_of[1], 1), -3, 0).astype(jnp.int32)
    weight_levels = draw_weight_levels(jax.random.fold_in(streams_of[5], 71), 0)
    column_scale = jnp.clip(jnp.exp(math.log(0.0043335953) - 2.3025851 * jax.random.uniform(streams_of[3], (D,), jnp.float32) ** steps_of(streams_of[3], (D,), ((0, 8),), -0.2, 0.2)), 0.00043335953, 0.0043335953)
    residual = gaussian(streams_of[4], (ROWS, D), 1.0, 6.0, ((0, 16), (1, 8)))
    return {"hidden": hidden, "exponents": exponents, "weight_levels": weight_levels, "column_scale": column_scale, "residual": residual}


def paley_table():
    members = [(a, b) for a in range(5) for b in range(5)]
    squares = set()
    for a, b in members:
        if (a, b) != (0, 0):
            squares.add(((a * a + 2 * b * b) % 5, 2 * a * b % 5))
    field_size = len(members)
    jacobsthal = np.zeros((field_size, field_size))
    for i, (a, b) in enumerate(members):
        for j, (c, d) in enumerate(members):
            difference = ((a - c) % 5, (b - d) % 5)
            if difference == (0, 0):
                jacobsthal[i, j] = 0.0
            elif difference in squares:
                jacobsthal[i, j] = 1.0
            else:
                jacobsthal[i, j] = -1.0
    conference = np.zeros((field_size + 1, field_size + 1))
    conference[0, 1:] = 1.0
    conference[1:, 0] = 1.0
    conference[1:, 1:] = jacobsthal
    hadamard = np.kron(conference, np.array([[1.0, -1.0], [-1.0, -1.0]]))
    hadamard = hadamard + np.kron(np.eye(field_size + 1), np.array([[1.0, 1.0], [1.0, -1.0]]))
    return hadamard

def sylvester(count):
    positions = jnp.arange(count, dtype=jnp.int32)
    common = jnp.bitwise_and(positions[:, None], positions[None, :])
    parity = jnp.zeros((count, count), jnp.int32)
    for offset in range(count.bit_length()):
        parity = parity + jnp.bitwise_and(jnp.right_shift(common, offset), 1)
    return (1 - 2 * jnp.bitwise_and(parity, 1)).astype(jnp.float32)

def reference(hidden, exponents, weight_levels, column_scale, residual):
    row_count = hidden.shape[0]
    blocks = FF // HAD_SMALL
    small_table = jnp.asarray(paley_table(), dtype=jnp.float32)
    large_table = sylvester(blocks)
    signal = hidden.astype(jnp.float32).reshape(row_count, blocks, HAD_SMALL)
    signal = jnp.einsum('rjk,kb->rjb', signal, small_table, precision=lax.Precision.HIGHEST)
    signal = jnp.einsum('rjb,ja->rab', signal, large_table, precision=lax.Precision.HIGHEST)
    rotated = signal.reshape(row_count, FF) * (1.0 / np.sqrt(FF))
    powers = jnp.exp2(exponents.astype(jnp.float32))
    inverse = jnp.exp2(-exponents.astype(jnp.float32))
    code_values = jnp.clip(rotated * inverse[:, None], -8.0, 7.0).astype(jnp.bfloat16)
    dequant = code_values * powers.astype(jnp.bfloat16)[:, None]
    totals = jnp.dot(dequant, weight_levels, preferred_element_type=jnp.float32)
    return (totals * column_scale[None, :] + residual.astype(jnp.float32)).astype(jnp.bfloat16)
```

```python
import math

import jax
import jax.numpy as jnp
import ml_dtypes
import numpy as np
from jax import lax
from jax.experimental import pallas as pl
from jax.experimental.pallas import tpu as pltpu
from jax.sharding import PartitionSpec as P

FF = 53248
HAD_SMALL = 52
WIDE = 1664
DP, TENSOR, RING = 8, 16, 4
ROWS = 128
WIDTH = 2 * WIDE
COLS = 2048
HALF = COLS // 2
CHUNKS = 4
PIECE = ROWS // CHUNKS
SUB = PIECE // 2
F32, BF16 = jnp.float32, jnp.bfloat16


def paley_table():
    members = [(a, b) for a in range(5) for b in range(5)]
    squares = set()
    for a, b in members:
        if (a, b) != (0, 0):
            squares.add(((a * a + 2 * b * b) % 5, 2 * a * b % 5))
    jacobsthal = np.zeros((25, 25))
    for i, (a, b) in enumerate(members):
        for j, (c, d) in enumerate(members):
            difference = ((a - c) % 5, (b - d) % 5)
            if difference != (0, 0):
                jacobsthal[i, j] = 1.0 if difference in squares else -1.0
    conference = np.zeros((26, 26))
    conference[0, 1:] = 1.0
    conference[1:, 0] = 1.0
    conference[1:, 1:] = jacobsthal
    hadamard = np.kron(conference, np.array([[1.0, -1.0], [-1.0, -1.0]]))
    return hadamard + np.kron(np.eye(26), np.array([[1.0, 1.0], [1.0, -1.0]]))


def sylvester(count):
    table = np.ones((1, 1))
    while table.shape[0] < count:
        table = np.kron(np.array([[1.0, 1.0], [1.0, -1.0]]), table)
    return table


def kernel(
    exponents, hidden_hbm, wide_hbm, weights_hbm, scale_hbm, residual_hbm, out,
    hidden, wide, weights, scale, residual,
    stage, got, stage_back, got_back, codes, sums,
    a1, a2, a3, a4, b1, b2, b3, b4,
    load_sem, out_send, out_recv, back_send, back_recv, own_sem,
    y_send, y_recv, pair_send, pair_recv, rs_send, rs_recv,
):
    d, t = lax.axis_index("dp"), lax.axis_index("tensor")
    z, x = lax.div(t, RING), lax.rem(t, RING)
    core = lax.rem(d, 2)

    def loads():
        pairs = [
            (hidden_hbm, hidden), (wide_hbm, wide), (weights_hbm, weights),
            (scale_hbm, scale), (residual_hbm, residual),
        ]
        return [pltpu.make_async_copy(src, dst, load_sem.at[i]) for i, (src, dst) in enumerate(pairs)]

    for load in loads():
        load.start()

    def dp_device(distance):
        return (lax.rem(d + 2 * distance + DP, DP), t)

    def pair_device():
        return (d + 1 - 2 * core, t)

    def plane_device(dz, dx):
        return (d, lax.rem(z + dz + RING, RING) * RING + lax.rem(x + dx + RING, RING))

    def offset_device(off):
        return plane_device(lax.div(off, RING), lax.rem(off, RING))

    def offset_source(off):
        return plane_device(-lax.div(off, RING), -lax.rem(off, RING))

    barrier = pltpu.get_barrier_semaphore()

    def greet(off, carry):
        pl.semaphore_signal(barrier, inc=1, device_id=offset_device(off), device_id_type=pl.DeviceIdType.MESH)
        return carry

    lax.fori_loop(1, TENSOR, greet, 0)
    for device in (dp_device(1), dp_device(-1), pair_device()):
        pl.semaphore_signal(barrier, inc=1, device_id=device, device_id_type=pl.DeviceIdType.MESH)

    def remote(src, dst, send, recv, device):
        return pltpu.make_async_remote_copy(
            src_ref=src, dst_ref=dst, send_sem=send, recv_sem=recv,
            device_id=device, device_id_type=pl.DeviceIdType.MESH,
        )

    loads()[0].wait()

    def split(pair, carry):
        at = pl.multiple_of(pair * 16, 16)
        block = hidden[pl.ds(at, 16), :].astype(F32)
        for i in range(2):
            rows = block[8 * i : 8 * i + 8]
            stage[2 * pair + i] = jnp.concatenate([rows[:, :WIDE], rows[:, WIDE:]], axis=0).astype(BF16)
        return carry

    lax.fori_loop(0, ROWS // 16, split, 0)
    pl.semaphore_wait(barrier, TENSOR - 1 + 3)

    def exchange(source, target, send, recv, own):
        def make(off):
            device = offset_device(off)
            return remote(source.at[device[1]], target.at[t], send.at[off], recv.at[off], device)

        def begin(off, carry):
            make(off).start()
            return carry

        def finish(off, carry):
            sender = offset_source(off)[1]
            remote(source.at[t], target.at[sender], send.at[off], recv.at[off], offset_device(off)).wait_recv()
            return carry

        def drain(off, carry):
            make(off).wait_send()
            return carry

        mine = pltpu.make_async_copy(source.at[t], target.at[t], own)
        mine.start()
        lax.fori_loop(1, TENSOR, begin, 0)

        def wait():
            mine.wait()
            lax.fori_loop(1, TENSOR, finish, 0)

        return wait, lambda: lax.fori_loop(1, TENSOR, drain, 0)

    out_wait, out_drain = exchange(stage, got, out_send, out_recv, own_sem.at[0])
    out_wait()
    loads()[1].wait()

    row = lax.broadcasted_iota(jnp.int32, (8, 1), 0)
    exponent = jnp.zeros((8, 1), jnp.int32)
    for r in range(8):
        exponent = jnp.where(row == r, exponents[t * 8 + r], exponent)
    power = jnp.left_shift(1, exponent + 3).astype(F32) * 0.125
    low, high = power * -8.0, power * 7.0

    def transform(at, size):
        left = got[...].reshape(TENSOR * 16, WIDE)
        product = jnp.dot(left, wide[:, pl.ds(at, size)], preferred_element_type=F32)
        parts = [product[8 * i : 8 * i + 8] for i in range(2 * TENSOR)]
        step = 1
        while step < len(parts):
            for i in range(len(parts)):
                if i & step == 0:
                    u, v = parts[i], parts[i + step]
                    parts[i], parts[i + step] = u + v, u - v
            step *= 2
        parts = [jnp.minimum(jnp.maximum(p * (1.0 / math.sqrt(FF)), low), high) for p in parts]
        for i in range(TENSOR):
            stage_back[i, :, pl.ds(at, size)] = jnp.concatenate(parts[2 * i : 2 * i + 2], axis=0).astype(BF16)

    def transform_step(i, carry):
        transform(pl.multiple_of(i * 256, 256), 256)
        return carry

    lax.fori_loop(0, WIDE // 256, transform_step, 0)
    transform(WIDE // 256 * 256, WIDE % 256)

    back_wait, back_drain = exchange(stage_back, got_back, back_send, back_recv, own_sem.at[1])
    out_drain()
    back_wait()

    for chunk in range(CHUNKS):
        for side in range(2):
            first = side * (TENSOR // 2) + 2 * chunk
            blocks = [got_back[first + i].astype(F32) for i in range(2)]
            for half in range(2):
                rows = jnp.concatenate([b[8 * half : 8 * half + 8] for b in blocks], axis=0)
                codes[chunk, d, side * SUB : side * SUB + SUB, half * WIDE : half * WIDE + WIDE] = rows.astype(BF16)
    back_drain()

    def index(distance):
        return lax.rem(d + 2 * distance + DP, DP)

    def whole(chunk, distance):
        return codes.at[chunk, index(distance)]

    def part(chunk, distance, side):
        return codes.at[chunk, index(distance), side * SUB : side * SUB + SUB]

    def y_copy(chunk, kind, receiving):
        sign = 1 if kind in (0, 2) else -1
        if kind < 2:
            ref = whole(chunk, -sign if receiving else 0)
        else:
            ref = part(chunk, -2 * sign if receiving else -sign, kind - 2)
        return remote(ref, ref, y_send.at[chunk, kind], y_recv.at[chunk, kind], dp_device(sign))

    def pair_copy(chunk, kind, receiving):
        def ref_of(base):
            if kind < 3:
                return codes.at[chunk, lax.rem(base + 2 * (0, -1, 1)[kind] + DP, DP)]
            return codes.at[chunk, lax.rem(base + 4, DP), (kind - 3) * SUB : (kind - 3) * SUB + SUB]

        ref = ref_of(pair_device()[0] if receiving else d)
        return remote(ref, ref, pair_send.at[chunk, kind], pair_recv.at[chunk, kind], pair_device())

    def send_own(chunk):
        for kind in range(2):
            y_copy(chunk, kind, False).start()
        pair_copy(chunk, 0, False).start()

    lanes = (slice(0, HALF), slice(HALF, COLS))
    bufs = ((a1, a2, a3, a4), (b1, b2, b3, b4))

    def group(chunk, path, target, side=None):
        span = slice(None) if side is None else slice(2 * side, 2 * side + 2)
        if path == 0:
            return (chunk, target, span, slice(None), lanes[path])
        return (chunk, span, target, slice(None), lanes[path])

    def block(chunk, path, target, side=None):
        width = HALF if side is None else HALF // 2
        begin = lanes[path].start + (0 if side is None else side * width)
        where = (z, target) if path == 0 else (target, x)
        return (chunk, *where, slice(None), slice(begin, begin + width))

    def axes(path, phase):
        along_z = (path == 0) == (phase == 0)
        if along_z:
            return z, lambda n: plane_device(n, 0)
        return x, lambda n: plane_device(0, n)

    def rs_copy(chunk, path, step, way):
        sign = 1 if way == 0 else -1
        here, device = axes(path, step // 2)
        pick = group if step < 2 else block
        if step % 2 == 0:
            src = sums.at[pick(chunk, path, lax.rem(here + 2, RING), way)]
        else:
            src = sums.at[pick(chunk, path, lax.rem(here + sign + RING, RING))]
        number = (path * 4 + step) * 2 + way
        return remote(
            src, bufs[path][step].at[chunk, way],
            rs_send.at[chunk, number], rs_recv.at[chunk, number], device(sign),
        )

    def rs_start(chunk, path, step):
        for way in range(2):
            rs_copy(chunk, path, step, way).start()

    def rs_wait(chunk, path, step):
        for way in range(2):
            rs_copy(chunk, path, step, way).wait_recv()

    def add_into(where, buffer):
        sums[where] = (sums[where].astype(F32) + buffer.astype(F32)).astype(BF16)

    def rs_second(chunk, path, phase):
        step = 2 * phase
        pick = group if phase == 0 else block
        here, _ = axes(path, phase)
        for way in range(2):
            sign = 1 if way == 0 else -1
            rs_copy(chunk, path, step, way).wait_recv()
            add_into(pick(chunk, path, lax.rem(here + sign + RING, RING), way), bufs[path][step][chunk, way])
            rs_copy(chunk, path, step + 1, way).start()

    def rs_third(chunk, path):
        rs_wait(chunk, path, 1)
        here, _ = axes(path, 0)
        where = group(chunk, path, here)
        buffer = bufs[path][1]
        total = sums[where].astype(F32) + buffer[chunk, 0].astype(F32) + buffer[chunk, 1].astype(F32)
        sums[where] = total.astype(BF16)
        rs_start(chunk, path, 2)

    def rs_finish(chunk, path):
        rs_wait(chunk, path, 3)
        here, _ = axes(path, 1)
        buffer = bufs[path][3]
        total = sums[block(chunk, path, here)].astype(F32) + buffer[chunk, 0].astype(F32) + buffer[chunk, 1].astype(F32)
        rows = slice(chunk * SUB, chunk * SUB + SUB)
        cols = lanes[path]
        out[rows, cols] = (total * scale[:, cols] + residual[rows, cols].astype(F32)).astype(BF16)

    def multiply(chunk, path):
        def tile(i, carry):
            at = pl.multiple_of(path * HALF + i * 512, 512)
            left = codes[chunk].reshape(DP * PIECE, WIDTH)
            product = jnp.dot(left, weights[:, pl.ds(at, 512)], preferred_element_type=F32)
            sums[chunk, :, :, :, pl.ds(at, 512)] = product.astype(BF16).reshape(RING, RING, SUB, 512)
            return carry

        lax.fori_loop(0, HALF // 512, tile, 0)

    send_own(0)
    send_own(1)
    for i in (2, 3, 4):
        loads()[i].wait()
    for chunk in range(CHUNKS + 1):
        live, late = chunk < CHUNKS, chunk > 0
        if live:
            for kind in range(2):
                y_copy(chunk, kind, True).wait_recv()
                y_copy(chunk, kind + 2, False).start()
                pair_copy(chunk, kind + 1, False).start()
            if chunk + 2 < CHUNKS:
                send_own(chunk + 2)
        if late:
            for path in range(2):
                rs_second(chunk - 1, path, 0)
        if live:
            for kind in range(2):
                y_copy(chunk, kind + 2, True).wait_recv()
                pair_copy(chunk, kind + 3, False).start()
        if late:
            for path in range(2):
                rs_third(chunk - 1, path)
        if live:
            for kind in range(5):
                pair_copy(chunk, kind, True).wait_recv()
            multiply(chunk, 0)
            rs_start(chunk, 0, 0)
        if late:
            for path in range(2):
                rs_second(chunk - 1, path, 1)
        if live:
            multiply(chunk, 1)
            rs_start(chunk, 1, 0)
        if late:
            for path in range(2):
                rs_finish(chunk - 1, path)
    for chunk in range(CHUNKS):
        for kind in range(4):
            y_copy(chunk, kind, False).wait_send()
        for kind in range(5):
            pair_copy(chunk, kind, False).wait_send()
        for path in range(2):
            for step in range(4):
                for way in range(2):
                    rs_copy(chunk, path, step, way).wait_send()


def shards(hidden, exponents, weight_levels, column_scale, residual):
    wide = np.kron(sylvester(32), paley_table()).astype(ml_dtypes.bfloat16)
    anywhere = pl.BlockSpec(memory_space=pl.ANY)
    dma = pltpu.SemaphoreType.DMA

    def vmem(*shape, dtype=BF16):
        return pltpu.VMEM(shape, dtype)

    return pl.pallas_call(
        kernel,
        out_shape=jax.ShapeDtypeStruct(residual.shape, BF16),
        in_specs=[pl.BlockSpec(memory_space=pltpu.SMEM)] + [anywhere] * 5,
        out_specs=pl.BlockSpec(memory_space=pltpu.VMEM),
        scratch_shapes=[
            vmem(ROWS, WIDTH), vmem(WIDE, WIDE), vmem(WIDTH, COLS), vmem(1, COLS, dtype=F32), vmem(ROWS // 2, COLS),
            *[vmem(TENSOR, 16, WIDE) for _ in range(4)],
            vmem(CHUNKS, DP, PIECE, WIDTH), vmem(CHUNKS, RING, RING, SUB, COLS),
            *[
                vmem(CHUNKS, 2, *shape)
                for _ in range(2)
                for shape in ((2, SUB, HALF), (RING, SUB, HALF), (SUB, HALF // 2), (SUB, HALF))
            ],
            dma((5,)), dma((TENSOR,)), dma((TENSOR,)), dma((TENSOR,)), dma((TENSOR,)), dma((2,)),
            dma((CHUNKS, 4)), dma((CHUNKS, 4)), dma((CHUNKS, 5)), dma((CHUNKS, 5)),
            dma((CHUNKS, 16)), dma((CHUNKS, 16)),
        ],
        compiler_params=pltpu.CompilerParams(
            collective_id=0, has_side_effects=True, vmem_limit_bytes=60 * 1024 * 1024,
        ),
        cost_estimate=pl.CostEstimate(flops=15_400_000_000, bytes_accessed=21_000_000, transcendentals=0),
    )(exponents, hidden, wide, weight_levels, column_scale.reshape(1, COLS), residual)


def solution(mesh):
    return jax.shard_map(
        shards,
        mesh=mesh,
        in_specs=(P("dp", "tensor"), P("dp"), P("tensor", "dp"), P("dp"), P("tensor", "dp")),
        out_specs=P("tensor", "dp"),
        check_vma=False,
    )
```

```python
import math

import jax
import jax.numpy as jnp
import ml_dtypes
import numpy as np
from jax import lax
from jax.experimental import pallas as pl
from jax.experimental.pallas import tpu as pltpu
from jax.sharding import PartitionSpec as P

FF = 53248
HAD_SMALL = 52
WIDE = 1664
DP, TENSOR, RING = 8, 16, 4
ROWS = 128
WIDTH = 2 * WIDE
COLS = 2048
HALF = COLS // 2
CHUNKS = 4
PIECE = ROWS // CHUNKS
SUB = PIECE // 2
F32, BF16 = jnp.float32, jnp.bfloat16


def paley_table():
    members = [(a, b) for a in range(5) for b in range(5)]
    squares = set()
    for a, b in members:
        if (a, b) != (0, 0):
            squares.add(((a * a + 2 * b * b) % 5, 2 * a * b % 5))
    jacobsthal = np.zeros((25, 25))
    for i, (a, b) in enumerate(members):
        for j, (c, d) in enumerate(members):
            difference = ((a - c) % 5, (b - d) % 5)
            if difference != (0, 0):
                jacobsthal[i, j] = 1.0 if difference in squares else -1.0
    conference = np.zeros((26, 26))
    conference[0, 1:] = 1.0
    conference[1:, 0] = 1.0
    conference[1:, 1:] = jacobsthal
    hadamard = np.kron(conference, np.array([[1.0, -1.0], [-1.0, -1.0]]))
    return hadamard + np.kron(np.eye(26), np.array([[1.0, 1.0], [1.0, -1.0]]))


def sylvester(count):
    table = np.ones((1, 1))
    while table.shape[0] < count:
        table = np.kron(np.array([[1.0, 1.0], [1.0, -1.0]]), table)
    return table


def kernel(
    exponents_hbm, hidden_hbm, wide_hbm, weights_hbm, scale_hbm, residual_hbm, out,
    exponents, hidden, wide, weights, scale, residual,
    stage, got, stage_back, got_back, codes, sums,
    a1, a2, a3, b1, b2, b3,
    load_sem, out_send, out_recv, back_send, back_recv, own_sem,
    y_send, y_recv, pair_send, pair_recv, rs_send, rs_recv,
):
    d, t = lax.axis_index("dp"), lax.axis_index("tensor")
    z, x = lax.div(t, RING), lax.rem(t, RING)
    core = lax.rem(d, 2)

    def loads():
        pairs = [
            (hidden_hbm, hidden), (wide_hbm, wide), (weights_hbm, weights),
            (scale_hbm, scale), (residual_hbm, residual), (exponents_hbm, exponents),
        ]
        return [pltpu.make_async_copy(src, dst, load_sem.at[i]) for i, (src, dst) in enumerate(pairs)]

    for load in loads():
        load.start()

    def dp_device(distance):
        return (lax.rem(d + 2 * distance + DP, DP), t)

    def pair_device():
        return (d + 1 - 2 * core, t)

    def plane_device(dz, dx):
        return (d, lax.rem(z + dz + RING, RING) * RING + lax.rem(x + dx + RING, RING))

    def offset_device(off):
        return plane_device(lax.div(off, RING), lax.rem(off, RING))

    def offset_source(off):
        return plane_device(-lax.div(off, RING), -lax.rem(off, RING))

    barrier = pltpu.get_barrier_semaphore()

    def greet(off, carry):
        pl.semaphore_signal(barrier, inc=1, device_id=offset_device(off), device_id_type=pl.DeviceIdType.MESH)
        return carry

    lax.fori_loop(1, TENSOR, greet, 0)
    for device in (dp_device(1), dp_device(-1), pair_device()):
        pl.semaphore_signal(barrier, inc=1, device_id=device, device_id_type=pl.DeviceIdType.MESH)

    def remote(src, dst, send, recv, device):
        return pltpu.make_async_remote_copy(
            src_ref=src, dst_ref=dst, send_sem=send, recv_sem=recv,
            device_id=device, device_id_type=pl.DeviceIdType.MESH,
        )

    def holder(chunk, side, i):
        return RING * (chunk % 2 * 2 + side) + 2 * i + (side + chunk // 2) % 2

    odd = lax.rem(z + x, 2)
    first_row = lax.rem(z, 2) * 64 + (2 * odd + lax.div(z, 2)) * 16 + lax.div(x, 2) * 8

    def split(chunk):
        for side in range(2):
            block = hidden[side * 64 + chunk * 16 : side * 64 + chunk * 16 + 16, :].astype(F32)
            for i in range(2):
                rows = block[8 * i : 8 * i + 8]
                stage[holder(chunk, side, i)] = jnp.concatenate([rows[:, :WIDE], rows[:, WIDE:]], axis=0).astype(BF16)

    def out_copy(off):
        device = offset_device(off)
        return remote(stage.at[device[1]], got.at[t], out_send.at[off], out_recv.at[off], device)

    def out_begin(parity):
        turn = lax.rem(odd + parity, 2)

        def begin(i, carry):
            dz = lax.div(i, 2)
            out_copy(RING * dz + 2 * lax.rem(i, 2) + lax.rem(dz + turn, 2)).start()
            return carry

        lax.fori_loop(1 - turn, 8, begin, 0)

    loads()[0].wait()
    split(0)
    split(1)
    pl.semaphore_wait(barrier, TENSOR - 1 + 3)
    out_begin(0)
    split(2)
    split(3)
    out_begin(1)
    mine = pltpu.make_async_copy(stage.at[t], got.at[t], own_sem.at[0])
    mine.start()
    mine.wait()

    def out_wait(off, carry):
        sender = offset_source(off)[1]
        remote(stage.at[t], got.at[sender], out_send.at[off], out_recv.at[off], offset_device(off)).wait_recv()
        return carry

    lax.fori_loop(1, TENSOR, out_wait, 0)
    loads()[1].wait()
    loads()[5].wait()

    row = lax.broadcasted_iota(jnp.int32, (8, 1), 0)
    exponent = jnp.zeros((8, 1), jnp.int32)
    for r in range(8):
        exponent = jnp.where(row == r, exponents[first_row + r], exponent)
    power = jnp.left_shift(1, exponent + 3).astype(F32) * 0.125
    low, high = power * -8.0, power * 7.0

    def transform(at, size):
        left = got[...].reshape(TENSOR * 16, WIDE)
        product = jnp.dot(left, wide[:, pl.ds(at, size)], preferred_element_type=F32)
        parts = [product[8 * i : 8 * i + 8] for i in range(2 * TENSOR)]
        step = 1
        while step < len(parts):
            for i in range(len(parts)):
                if i & step == 0:
                    u, v = parts[i], parts[i + step]
                    parts[i], parts[i + step] = u + v, u - v
            step *= 2
        parts = [jnp.minimum(jnp.maximum(p * (1.0 / math.sqrt(FF)), low), high) for p in parts]
        for i in range(TENSOR):
            stage_back[i, :, pl.ds(at, size)] = jnp.concatenate(parts[2 * i : 2 * i + 2], axis=0).astype(BF16)

    spans = ((0, 768), (768, WIDE - 768))

    def back_copy(piece, off):
        device = offset_device(off)
        lanes = pl.ds(*spans[piece])
        return remote(
            stage_back.at[device[1], :, lanes], got_back.at[t, :, lanes],
            back_send.at[piece, off], back_recv.at[piece, off], device,
        )

    for piece in range(2):
        begin, size = spans[piece]

        def transform_step(i, carry):
            transform(pl.multiple_of(begin + i * 256, 256), 256)
            return carry

        lax.fori_loop(0, size // 256, transform_step, 0)
        if size % 256:
            transform(begin + size // 256 * 256, size % 256)

        def back_begin(off, carry):
            back_copy(piece, off).start()
            return carry

        lax.fori_loop(1, TENSOR, back_begin, 0)
        lanes = pl.ds(begin, size)
        pltpu.make_async_copy(stage_back.at[t, :, lanes], got_back.at[t, :, lanes], own_sem.at[1 + piece]).start()

    for piece in range(2):
        lanes = pl.ds(*spans[piece])
        pltpu.make_async_copy(stage_back.at[t, :, lanes], got_back.at[t, :, lanes], own_sem.at[1 + piece]).wait()

    def back_wait(sender):
        off = lax.rem(z - sender // RING + RING, RING) * RING + lax.rem(x - sender % RING + RING, RING)

        @pl.when(off > 0)
        def _():
            for piece in range(2):
                lanes = pl.ds(*spans[piece])
                remote(
                    stage_back.at[t, :, lanes], got_back.at[sender, :, lanes],
                    back_send.at[piece, off], back_recv.at[piece, off], offset_device(off),
                ).wait_recv()

    def collect(chunk):
        for side in range(2):
            senders = [holder(chunk, side, i) for i in range(2)]
            for sender in senders:
                back_wait(sender)
            blocks = [got_back[sender].astype(F32) for sender in senders]
            for half in range(2):
                rows = jnp.concatenate([b[8 * half : 8 * half + 8] for b in blocks], axis=0)
                codes[chunk, d, side * SUB : side * SUB + SUB, half * WIDE : half * WIDE + WIDE] = rows.astype(BF16)
        pair_copy(chunk, 0, False).start()

    def index(distance):
        return lax.rem(d + 2 * distance + DP, DP)

    def whole(chunk, distance):
        return codes.at[chunk, index(distance)]

    def part(chunk, distance, side):
        return codes.at[chunk, index(distance), side * SUB : side * SUB + SUB]

    def y_copy(chunk, kind, receiving):
        sign = 1 if kind in (0, 2) else -1
        if kind < 2:
            ref = whole(chunk, -sign if receiving else 0)
        else:
            ref = part(chunk, -2 * sign if receiving else -sign, kind - 2)
        return remote(ref, ref, y_send.at[chunk, kind], y_recv.at[chunk, kind], dp_device(sign))

    def pair_copy(chunk, kind, receiving):
        def ref_of(base):
            if kind < 3:
                return codes.at[chunk, lax.rem(base + 2 * (0, -1, 1)[kind] + DP, DP)]
            return codes.at[chunk, lax.rem(base + 4, DP), (kind - 3) * SUB : (kind - 3) * SUB + SUB]

        ref = ref_of(pair_device()[0] if receiving else d)
        return remote(ref, ref, pair_send.at[chunk, kind], pair_recv.at[chunk, kind], pair_device())

    def send_own(chunk):
        for kind in range(2):
            y_copy(chunk, kind, False).start()

    lanes = (slice(0, HALF), slice(HALF, COLS))
    bufs = ((a1, a2, a3), (b1, b2, b3))

    def group(chunk, path, target, side=None):
        span = slice(None) if side is None else slice(2 * side, 2 * side + 2)
        if path == 0:
            return (chunk, target, span, slice(None), lanes[path])
        return (chunk, span, target, slice(None), lanes[path])

    def block(chunk, path, target):
        where = (z, target) if path == 0 else (target, x)
        return (chunk, *where, slice(None), lanes[path])

    def axes(path, phase):
        along_z = (path == 0) == (phase == 0)
        if along_z:
            return z, lambda n: plane_device(n, 0)
        return x, lambda n: plane_device(0, n)

    def rs_copy(chunk, path, step, way):
        sign = (1, -1, 2)[way]
        here, device = axes(path, step // 2)
        target = lax.rem(here + (2 if step == 0 else sign) + RING, RING)
        if step == 0:
            src = sums.at[group(chunk, path, target, way)]
        elif step == 1:
            src = sums.at[group(chunk, path, target)]
        else:
            src = sums.at[block(chunk, path, target)]
        number = path * 7 + step * 2 + way
        return remote(
            src, bufs[path][step].at[chunk, way],
            rs_send.at[chunk, number], rs_recv.at[chunk, number], device(sign),
        )

    def rs_start(chunk, path, step):
        for way in range(3 if step == 2 else 2):
            rs_copy(chunk, path, step, way).start()

    def rs_second(chunk, path):
        here, _ = axes(path, 0)
        for way in range(2):
            rs_copy(chunk, path, 0, way).wait_recv()
            where = group(chunk, path, lax.rem(here + (1, -1)[way] + RING, RING), way)
            sums[where] = (sums[where].astype(F32) + bufs[path][0][chunk, way].astype(F32)).astype(BF16)
            rs_copy(chunk, path, 1, way).start()

    def rs_third(chunk, path):
        where = group(chunk, path, axes(path, 0)[0])
        total = sums[where].astype(F32)
        for way in range(2):
            rs_copy(chunk, path, 1, way).wait_recv()
            total += bufs[path][1][chunk, way].astype(F32)
        sums[where] = total.astype(BF16)
        rs_start(chunk, path, 2)

    def rs_finish(chunk, path):
        total = sums[block(chunk, path, axes(path, 1)[0])].astype(F32)
        for way in range(3):
            rs_copy(chunk, path, 2, way).wait_recv()
            total += bufs[path][2][chunk, way].astype(F32)
        rows, cols = slice(chunk * SUB, chunk * SUB + SUB), lanes[path]
        out[rows, cols] = (total * scale[:, cols] + residual[rows, cols].astype(F32)).astype(BF16)

    height = lax.div(d, 2)

    def multiply_own(path):
        def tile(i, carry):
            at = pl.multiple_of(path * HALF + i * 512, 512)
            left = codes[:, pl.ds(2 * height, 2)].reshape(CHUNKS * 2 * PIECE, WIDTH)
            product = jnp.dot(left, weights[:, pl.ds(at, 512)], preferred_element_type=F32)
            sums[:, height, :, :, pl.ds(at, 512)] = product.astype(BF16).reshape(CHUNKS, RING, SUB, 512)
            return carry

        lax.fori_loop(0, HALF // 512, tile, 0)

    def multiply(chunk, path):
        others = [lax.rem(height + i, RING) for i in range(1, RING)]

        def tile(i, carry):
            at = pl.multiple_of(path * HALF + i * 512, 512)
            left = jnp.concatenate([codes[chunk, pl.ds(2 * o, 2)].reshape(2 * PIECE, WIDTH) for o in others], axis=0)
            product = jnp.dot(left, weights[:, pl.ds(at, 512)], preferred_element_type=F32).astype(BF16)
            for j, o in enumerate(others):
                rows = product[j * 2 * PIECE : (j + 1) * 2 * PIECE]
                sums[chunk, o, :, :, pl.ds(at, 512)] = rows.reshape(RING, SUB, 512)
            return carry

        lax.fori_loop(0, HALF // 512, tile, 0)

    def near(chunk):
        for kind in range(2):
            y_copy(chunk, kind, True).wait_recv()
            y_copy(chunk, kind + 2, False).start()
            pair_copy(chunk, kind + 1, False).start()

    def far(chunk):
        for kind in range(2):
            y_copy(chunk, kind + 2, True).wait_recv()
            pair_copy(chunk, kind + 3, False).start()

    def own(path):
        if path == 0:
            for i in (2, 3, 4):
                loads()[i].wait()
            for chunk in range(CHUNKS):
                pair_copy(chunk, 0, True).wait_recv()
        multiply_own(path)

    def product(chunk, path):
        if path == 0:
            for kind in range(1, 5):
                pair_copy(chunk, kind, True).wait_recv()
        multiply(chunk, path)
        rs_start(chunk, path, 0)

    def reduce(chunk, path, step):
        (rs_second, rs_third, None, rs_finish)[step - 2](chunk, path)

    collect(0)
    send_own(0)
    collect(1)
    collect(2)
    collect(3)
    send_own(1)
    near(0)
    own(0)
    send_own(2)
    own(1)
    near(1)
    send_own(3)
    far(0)
    product(0, 0)
    product(0, 1)
    near(2)
    far(1)
    reduce(0, 0, 2)
    reduce(0, 1, 2)
    product(1, 0)
    product(1, 1)
    near(3)
    reduce(0, 0, 3)
    reduce(0, 1, 3)
    far(2)
    reduce(1, 0, 2)
    reduce(1, 1, 2)
    product(2, 0)
    far(3)
    product(2, 1)
    product(3, 0)
    reduce(1, 0, 3)
    product(3, 1)
    reduce(2, 0, 2)
    reduce(2, 1, 2)
    reduce(3, 0, 2)
    reduce(3, 1, 2)
    reduce(1, 1, 3)
    reduce(2, 1, 3)
    reduce(1, 0, 5)
    reduce(2, 0, 3)
    reduce(0, 1, 5)
    reduce(0, 0, 5)
    reduce(3, 0, 3)
    reduce(3, 1, 3)
    reduce(2, 1, 5)
    reduce(1, 1, 5)
    reduce(2, 0, 5)
    reduce(3, 0, 5)
    reduce(3, 1, 5)

    def drain(off, carry):
        out_copy(off).wait_send()
        for piece in range(2):
            back_copy(piece, off).wait_send()
        return carry

    lax.fori_loop(1, TENSOR, drain, 0)
    for chunk in range(CHUNKS):
        for kind in range(4):
            y_copy(chunk, kind, False).wait_send()
        for kind in range(5):
            pair_copy(chunk, kind, False).wait_send()
        for path in range(2):
            for step in range(3):
                for way in range(3 if step == 2 else 2):
                    rs_copy(chunk, path, step, way).wait_send()


def shards(hidden, exponents, weight_levels, column_scale, residual):
    wide = np.kron(sylvester(32), paley_table()).astype(ml_dtypes.bfloat16)
    anywhere = pl.BlockSpec(memory_space=pl.ANY)
    dma = pltpu.SemaphoreType.DMA

    def vmem(*shape, dtype=BF16):
        return pltpu.VMEM(shape, dtype)

    return pl.pallas_call(
        kernel,
        out_shape=jax.ShapeDtypeStruct(residual.shape, BF16),
        in_specs=[anywhere] * 6,
        out_specs=pl.BlockSpec(memory_space=pltpu.VMEM),
        scratch_shapes=[
            pltpu.SMEM((ROWS,), jnp.int32), vmem(ROWS, WIDTH), vmem(WIDE, WIDE), vmem(WIDTH, COLS), vmem(1, COLS, dtype=F32), vmem(ROWS // 2, COLS),
            *[vmem(TENSOR, 16, WIDE) for _ in range(4)],
            vmem(CHUNKS, DP, PIECE, WIDTH), vmem(CHUNKS, RING, RING, SUB, COLS),
            *[
                vmem(CHUNKS, *shape)
                for _ in range(2)
                for shape in ((2, 2, SUB, HALF), (2, RING, SUB, HALF), (3, SUB, HALF))
            ],
            dma((6,)), dma((TENSOR,)), dma((TENSOR,)), dma((2, TENSOR)), dma((2, TENSOR)), dma((3,)),
            dma((CHUNKS, 4)), dma((CHUNKS, 4)), dma((CHUNKS, 5)), dma((CHUNKS, 5)),
            dma((CHUNKS, 14)), dma((CHUNKS, 14)),
        ],
        compiler_params=pltpu.CompilerParams(
            collective_id=0, has_side_effects=True, vmem_limit_bytes=60 * 1024 * 1024,
        ),
        cost_estimate=pl.CostEstimate(flops=15_400_000_000, bytes_accessed=21_000_000, transcendentals=0),
    )(exponents, hidden, wide, weight_levels, column_scale.reshape(1, COLS), residual)


def solution(mesh):
    return jax.shard_map(
        shards,
        mesh=mesh,
        in_specs=(P("dp", "tensor"), P("dp"), P("tensor", "dp"), P("dp"), P("tensor", "dp")),
        out_specs=P("tensor", "dp"),
        check_vma=False,
    )
```

```python
import math

import jax
import jax.numpy as jnp
import ml_dtypes
import numpy as np
from jax import lax
from jax.experimental import pallas as pl
from jax.experimental.pallas import tpu as pltpu
from jax.sharding import PartitionSpec as P

FF = 53248
HAD_SMALL = 52
WIDE = 1664
DP, TENSOR, RING = 8, 16, 4
ROWS = 128
WIDTH = 2 * WIDE
COLS = 2048
PATHS = 2
PART = COLS // PATHS
CHUNKS = 4
PIECE = ROWS // CHUNKS
SUB = PIECE // 2
F32, BF16 = jnp.float32, jnp.bfloat16


def paley_table():
    members = [(a, b) for a in range(5) for b in range(5)]
    squares = set()
    for a, b in members:
        if (a, b) != (0, 0):
            squares.add(((a * a + 2 * b * b) % 5, 2 * a * b % 5))
    jacobsthal = np.zeros((25, 25))
    for i, (a, b) in enumerate(members):
        for j, (c, d) in enumerate(members):
            difference = ((a - c) % 5, (b - d) % 5)
            if difference != (0, 0):
                jacobsthal[i, j] = 1.0 if difference in squares else -1.0
    conference = np.zeros((26, 26))
    conference[0, 1:] = 1.0
    conference[1:, 0] = 1.0
    conference[1:, 1:] = jacobsthal
    hadamard = np.kron(conference, np.array([[1.0, -1.0], [-1.0, -1.0]]))
    return hadamard + np.kron(np.eye(26), np.array([[1.0, 1.0], [1.0, -1.0]]))


def sylvester(count):
    table = np.ones((1, 1))
    while table.shape[0] < count:
        table = np.kron(np.array([[1.0, 1.0], [1.0, -1.0]]), table)
    return table


def kernel(
    exponents_hbm, hidden_hbm, wide_hbm, weights_hbm, scale_hbm, residual_hbm, out,
    exponents, hidden, wide, weights, scale, residual,
    stage, got, stage_back, got_back, codes, sums,
    arrived_1, arrived_2, arrived_3,
    load_sem, out_send, out_recv, back_send, back_recv, own_sem,
    y_send, y_recv, pair_send, pair_recv, rs_send, rs_recv,
):
    d, t = lax.axis_index("dp"), lax.axis_index("tensor")
    z, x = lax.div(t, RING), lax.rem(t, RING)
    core = lax.rem(d, 2)

    def loads():
        pairs = [
            (hidden_hbm, hidden), (wide_hbm, wide), (weights_hbm, weights),
            (scale_hbm, scale), (residual_hbm, residual), (exponents_hbm, exponents),
        ]
        return [pltpu.make_async_copy(src, dst, load_sem.at[i]) for i, (src, dst) in enumerate(pairs)]

    def dp_device(distance):
        return (lax.rem(d + 2 * distance + DP, DP), t)

    def pair_device():
        return (d + 1 - 2 * core, t)

    def plane_device(dz, dx):
        return (d, lax.rem(z + dz + RING, RING) * RING + lax.rem(x + dx + RING, RING))

    def offset_device(off):
        return plane_device(lax.div(off, RING), lax.rem(off, RING))

    def offset_source(off):
        return plane_device(-lax.div(off, RING), -lax.rem(off, RING))

    barrier = pltpu.get_barrier_semaphore()

    far_first = sorted(range(1, TENSOR), key=lambda off: -(min(off // RING, RING - off // RING) + min(off % RING, RING - off % RING)))
    for device in [plane_device(off // RING, off % RING) for off in far_first] + [dp_device(1), dp_device(-1), pair_device()]:
        pl.semaphore_signal(barrier, inc=1, device_id=device, device_id_type=pl.DeviceIdType.MESH)
    for load in loads():
        load.start()

    def remote(src, dst, send, recv, device):
        return pltpu.make_async_remote_copy(
            src_ref=src, dst_ref=dst, send_sem=send, recv_sem=recv,
            device_id=device, device_id_type=pl.DeviceIdType.MESH,
        )

    def holder(chunk, side, i):
        return RING * (chunk % 2 * 2 + side) + 2 * i + (side + chunk // 2) % 2

    odd = lax.rem(z + x, 2)
    first_row = lax.rem(z, 2) * 64 + (2 * odd + lax.div(z, 2)) * 16 + lax.div(x, 2) * 8

    def split(chunk):
        for side in range(2):
            block = hidden[side * 64 + chunk * 16 : side * 64 + chunk * 16 + 16, :].astype(F32)
            for i in range(2):
                rows = block[8 * i : 8 * i + 8]
                stage[holder(chunk, side, i)] = jnp.concatenate([rows[:, :WIDE], rows[:, WIDE:]], axis=0).astype(BF16)

    def out_copy(off):
        device = offset_device(off)
        return remote(stage.at[device[1]], got.at[t], out_send.at[off], out_recv.at[off], device)

    def out_begin(parity):
        turn = lax.rem(odd + parity, 2)

        def begin(i, carry):
            dz = lax.div(i, 2)
            out_copy(RING * dz + 2 * lax.rem(i, 2) + lax.rem(dz + turn, 2)).start()
            return carry

        lax.fori_loop(1 - turn, 8, begin, 0)

    loads()[0].wait()
    split(0)
    split(1)
    pl.semaphore_wait(barrier, TENSOR - 1 + 3)
    out_begin(0)
    split(2)
    split(3)
    out_begin(1)
    mine = pltpu.make_async_copy(stage.at[t], got.at[t], own_sem.at[0])
    mine.start()
    mine.wait()

    def out_wait(off, carry):
        sender = offset_source(off)[1]
        remote(stage.at[t], got.at[sender], out_send.at[off], out_recv.at[off], offset_device(off)).wait_recv()
        return carry

    lax.fori_loop(1, TENSOR, out_wait, 0)
    loads()[1].wait()
    loads()[5].wait()

    row = lax.broadcasted_iota(jnp.int32, (8, 1), 0)
    exponent = jnp.zeros((8, 1), jnp.int32)
    for r in range(8):
        exponent = jnp.where(row == r, exponents[first_row + r], exponent)
    power = jnp.left_shift(1, exponent + 3).astype(F32) * 0.125
    low, high = power * -8.0, power * 7.0

    def transform(at, size):
        left = got[...].reshape(TENSOR * 16, WIDE)
        product = jnp.dot(left, wide[:, pl.ds(at, size)], preferred_element_type=F32)
        parts = [product[8 * i : 8 * i + 8] for i in range(2 * TENSOR)]
        step = 1
        while step < len(parts):
            for i in range(len(parts)):
                if i & step == 0:
                    u, v = parts[i], parts[i + step]
                    parts[i], parts[i + step] = u + v, u - v
            step *= 2
        parts = [jnp.minimum(jnp.maximum(p * (1.0 / math.sqrt(FF)), low), high) for p in parts]
        for i in range(TENSOR):
            stage_back[i, :, pl.ds(at, size)] = jnp.concatenate(parts[2 * i : 2 * i + 2], axis=0).astype(BF16)

    spans = ((0, 768), (768, WIDE - 768))

    def back_copy(piece, off):
        device = offset_device(off)
        lanes = pl.ds(*spans[piece])
        return remote(
            stage_back.at[device[1], :, lanes], got_back.at[t, :, lanes],
            back_send.at[piece, off], back_recv.at[piece, off], device,
        )

    for piece in range(2):
        begin, size = spans[piece]

        def transform_step(i, carry):
            transform(pl.multiple_of(begin + i * 256, 256), 256)
            return carry

        lax.fori_loop(0, size // 256, transform_step, 0)
        if size % 256:
            transform(begin + size // 256 * 256, size % 256)

        def back_begin(off, carry):
            back_copy(piece, off).start()
            return carry

        lax.fori_loop(1, TENSOR, back_begin, 0)
        lanes = pl.ds(begin, size)
        pltpu.make_async_copy(stage_back.at[t, :, lanes], got_back.at[t, :, lanes], own_sem.at[1 + piece]).start()

    for piece in range(2):
        lanes = pl.ds(*spans[piece])
        pltpu.make_async_copy(stage_back.at[t, :, lanes], got_back.at[t, :, lanes], own_sem.at[1 + piece]).wait()

    def back_wait(sender):
        off = lax.rem(z - sender // RING + RING, RING) * RING + lax.rem(x - sender % RING + RING, RING)

        @pl.when(off > 0)
        def _():
            for piece in range(2):
                lanes = pl.ds(*spans[piece])
                remote(
                    stage_back.at[t, :, lanes], got_back.at[sender, :, lanes],
                    back_send.at[piece, off], back_recv.at[piece, off], offset_device(off),
                ).wait_recv()

    def collect(chunk):
        for side in range(2):
            senders = [holder(chunk, side, i) for i in range(2)]
            for sender in senders:
                back_wait(sender)
            blocks = [got_back[sender].astype(F32) for sender in senders]
            for half in range(2):
                rows = jnp.concatenate([b[8 * half : 8 * half + 8] for b in blocks], axis=0)
                codes[chunk, d, side * SUB : side * SUB + SUB, half * WIDE : half * WIDE + WIDE] = rows.astype(BF16)
        pair_copy(chunk, 0, False).start()

    def index(distance):
        return lax.rem(d + 2 * distance + DP, DP)

    def whole(chunk, distance):
        return codes.at[chunk, index(distance)]

    def part(chunk, distance, side):
        return codes.at[chunk, index(distance), side * SUB : side * SUB + SUB]

    def y_copy(chunk, kind, receiving):
        sign = -1 if kind % 2 else 1
        distance = -sign if kind in (2, 3) else 0
        ref = part(chunk, distance - sign if receiving else distance, kind % 2 if kind < 4 else 5 - kind)
        return remote(ref, ref, y_send.at[chunk, kind], y_recv.at[chunk, kind], dp_device(sign))

    def pair_copy(chunk, kind, receiving):
        def ref_of(base):
            if kind < 3:
                return codes.at[chunk, lax.rem(base + 2 * (0, -1, 1)[kind] + DP, DP)]
            return codes.at[chunk, lax.rem(base + 4, DP), (kind - 3) * SUB : (kind - 3) * SUB + SUB]

        ref = ref_of(pair_device()[0] if receiving else d)
        return remote(ref, ref, pair_send.at[chunk, kind], pair_recv.at[chunk, kind], pair_device())

    def send_own(chunk):
        for kind in (0, 1, 4, 5):
            y_copy(chunk, kind, False).start()

    def z_first(path):
        return path < PATHS // 2

    lanes = [slice(path * PART, path * PART + PART) for path in range(PATHS)]
    bufs = (arrived_1, arrived_2, arrived_3)

    def group(chunk, path, target, side=None):
        return (chunk, path, target, slice(None) if side is None else slice(2 * side, 2 * side + 2))

    def block(chunk, path, target):
        return (chunk, path, z if z_first(path) else x, target)

    def axes(path, phase):
        along_z = z_first(path) == (phase == 0)
        if along_z:
            return z, lambda n: plane_device(n, 0)
        return x, lambda n: plane_device(0, n)

    def rs_copy(chunk, path, step, way):
        sign = (1, -1, 2)[way]
        here, device = axes(path, step // 2)
        target = lax.rem(here + (2 if step == 0 else sign) + RING, RING)
        if step == 0:
            src = sums.at[group(chunk, path, target, way)]
        elif step == 1:
            src = sums.at[group(chunk, path, target)]
        else:
            src = sums.at[block(chunk, path, target)]
        number = path * 7 + step * 2 + way
        return remote(
            src, bufs[step].at[chunk, path, way],
            rs_send.at[chunk, number], rs_recv.at[chunk, number], device(sign),
        )

    def rs_start(chunk, path, step):
        for way in range(3 if step == 2 else 2):
            rs_copy(chunk, path, step, way).start()

    def rs_second(chunk, path):
        here, _ = axes(path, 0)
        for way in range(2):
            rs_copy(chunk, path, 0, way).wait_recv()
            where = group(chunk, path, lax.rem(here + (1, -1)[way] + RING, RING), way)
            sums[where] = (sums[where].astype(F32) + bufs[0][chunk, path, way].astype(F32)).astype(BF16)
            rs_copy(chunk, path, 1, way).start()

    def rs_third(chunk, path):
        where = group(chunk, path, axes(path, 0)[0])
        total = sums[where].astype(F32)
        for way in range(2):
            rs_copy(chunk, path, 1, way).wait_recv()
            total += bufs[1][chunk, path, way].astype(F32)
        sums[where] = total.astype(BF16)
        rs_start(chunk, path, 2)

    def rs_finish(chunk, path):
        total = sums[block(chunk, path, axes(path, 1)[0])].astype(F32)
        for way in range(3):
            rs_copy(chunk, path, 2, way).wait_recv()
            total += bufs[2][chunk, path, way].astype(F32)
        rows, cols = slice(chunk * SUB, chunk * SUB + SUB), lanes[path]
        out[rows, cols] = (total * scale[:, cols] + residual[rows, cols].astype(F32)).astype(BF16)

    height = lax.div(d, 2)

    def multiply_own(path):
        def tile(i, carry):
            at = pl.multiple_of(i * 512, 512)
            left = codes[:, pl.ds(2 * height, 2)].reshape(CHUNKS * 2 * PIECE, WIDTH)
            product = jnp.dot(left, weights[:, pl.ds(path * PART + at, 512)], preferred_element_type=F32)
            rows = product.astype(BF16).reshape(CHUNKS, RING, SUB, 512)
            if z_first(path):
                sums[:, path, height, :, :, pl.ds(at, 512)] = rows
            else:
                sums[:, path, :, height, :, pl.ds(at, 512)] = rows
            return carry

        lax.fori_loop(0, PART // 512, tile, 0)

    def multiply(chunk, path):
        others = [lax.rem(height + i, RING) for i in range(1, RING)]

        def tile(i, carry):
            at = pl.multiple_of(i * 512, 512)
            left = jnp.concatenate([codes[chunk, pl.ds(2 * o, 2)].reshape(2 * PIECE, WIDTH) for o in others], axis=0)
            product = jnp.dot(left, weights[:, pl.ds(path * PART + at, 512)], preferred_element_type=F32).astype(BF16)
            for j, o in enumerate(others):
                rows = product[j * 2 * PIECE : (j + 1) * 2 * PIECE].reshape(RING, SUB, 512)
                if z_first(path):
                    sums[chunk, path, o, :, :, pl.ds(at, 512)] = rows
                else:
                    sums[chunk, path, :, o, :, pl.ds(at, 512)] = rows
            return carry

        lax.fori_loop(0, PART // 512, tile, 0)

    def near(chunk):
        for kind in range(2):
            y_copy(chunk, kind, True).wait_recv()
            y_copy(chunk, kind + 2, False).start()

    def rest(chunk):
        for kind in range(2):
            y_copy(chunk, kind + 4, True).wait_recv()
            pair_copy(chunk, kind + 1, False).start()

    def far(chunk):
        for kind in range(2):
            y_copy(chunk, kind + 2, True).wait_recv()
            pair_copy(chunk, kind + 3, False).start()

    def own(path):
        if path == 0:
            for i in (2, 3, 4):
                loads()[i].wait()
            for chunk in range(CHUNKS):
                pair_copy(chunk, 0, True).wait_recv()
        multiply_own(path)

    def product(chunk, path):
        if path == 0:
            for kind in range(1, 5):
                pair_copy(chunk, kind, True).wait_recv()
        multiply(chunk, path)
        rs_start(chunk, path, 0)

    def reduce(chunk, path, step):
        (rs_second, rs_third, None, rs_finish)[step - 2](chunk, path)

    def drain(off, carry):
        out_copy(off).wait_send()
        for piece in range(2):
            back_copy(piece, off).wait_send()
        return carry

    def sent(chunk):
        for kind in range(6):
            y_copy(chunk, kind, False).wait_send()
        for kind in range(5):
            pair_copy(chunk, kind, False).wait_send()

    def passed(chunk, steps):
        for path in range(PATHS):
            for step in steps:
                for way in range(3 if step == 2 else 2):
                    rs_copy(chunk, path, step, way).wait_send()

    collect(0)
    send_own(0)
    collect(1)
    collect(2)
    collect(3)
    near(0)
    lax.fori_loop(1, TENSOR, drain, 0)
    own(0)
    send_own(1)
    own(1)
    rest(0)
    far(0)
    near(1)
    send_own(2)
    product(0, 0)
    product(0, 1)
    rest(1)
    far(1)
    reduce(0, 0, 2)
    near(2)
    send_own(3)
    reduce(0, 1, 2)
    product(1, 0)
    rest(2)
    product(1, 1)
    far(2)
    reduce(1, 0, 2)
    near(3)
    reduce(0, 0, 3)
    reduce(0, 1, 3)
    product(2, 0)
    reduce(1, 1, 2)
    rest(3)
    product(2, 1)
    far(3)
    reduce(1, 0, 3)
    product(3, 0)
    product(3, 1)
    reduce(2, 0, 2)
    reduce(2, 1, 2)
    reduce(3, 0, 2)
    reduce(0, 0, 5)
    reduce(3, 1, 2)
    reduce(2, 0, 3)
    reduce(1, 1, 3)
    reduce(1, 0, 5)
    reduce(2, 1, 3)
    reduce(3, 0, 3)
    reduce(3, 1, 3)
    reduce(1, 1, 5)
    reduce(0, 1, 5)
    reduce(2, 1, 5)
    reduce(2, 0, 5)
    reduce(3, 0, 5)
    reduce(3, 1, 5)
    for chunk in range(CHUNKS):
        sent(chunk)
        passed(chunk, (0, 1, 2))


def shards(hidden, exponents, weight_levels, column_scale, residual):
    wide = np.kron(sylvester(32), paley_table()).astype(ml_dtypes.bfloat16)
    anywhere = pl.BlockSpec(memory_space=pl.ANY)
    dma = pltpu.SemaphoreType.DMA

    def vmem(*shape, dtype=BF16):
        return pltpu.VMEM(shape, dtype)

    return pl.pallas_call(
        kernel,
        out_shape=jax.ShapeDtypeStruct(residual.shape, BF16),
        in_specs=[anywhere] * 6,
        out_specs=pl.BlockSpec(memory_space=pltpu.VMEM),
        scratch_shapes=[
            pltpu.SMEM((ROWS,), jnp.int32), vmem(ROWS, WIDTH), vmem(WIDE, WIDE), vmem(WIDTH, COLS), vmem(1, COLS, dtype=F32), vmem(ROWS // 2, COLS),
            *[vmem(TENSOR, 16, WIDE) for _ in range(4)],
            vmem(CHUNKS, DP, PIECE, WIDTH), vmem(CHUNKS, PATHS, RING, RING, SUB, PART),
            *[
                vmem(CHUNKS, PATHS, *shape)
                for shape in ((2, 2, SUB, PART), (2, RING, SUB, PART), (3, SUB, PART))
            ],
            dma((6,)), dma((TENSOR,)), dma((TENSOR,)), dma((2, TENSOR)), dma((2, TENSOR)), dma((3,)),
            dma((CHUNKS, 6)), dma((CHUNKS, 6)), dma((CHUNKS, 5)), dma((CHUNKS, 5)),
            dma((CHUNKS, 7 * PATHS)), dma((CHUNKS, 7 * PATHS)),
        ],
        compiler_params=pltpu.CompilerParams(
            collective_id=0, has_side_effects=True, vmem_limit_bytes=60 * 1024 * 1024,
        ),
        cost_estimate=pl.CostEstimate(flops=15_400_000_000, bytes_accessed=21_000_000, transcendentals=0),
    )(exponents, hidden, wide, weight_levels, column_scale.reshape(1, COLS), residual)


def solution(mesh):
    return jax.shard_map(
        shards,
        mesh=mesh,
        in_specs=(P("dp", "tensor"), P("dp"), P("tensor", "dp"), P("dp"), P("tensor", "dp")),
        out_specs=P("tensor", "dp"),
        check_vma=False,
    )
```

```python
import math

import jax
import jax.numpy as jnp
import ml_dtypes
import numpy as np
from jax import lax
from jax.experimental import pallas as pl
from jax.experimental.pallas import tpu as pltpu
from jax.sharding import PartitionSpec as P

FF = 53248
HAD_SMALL = 52
WIDE = 1664
DP, TENSOR, RING = 8, 16, 4
ROWS = 128
WIDTH = 2 * WIDE
COLS = 2048
PATHS = 2
PART = COLS // PATHS
CHUNKS = 4
PIECE = ROWS // CHUNKS
SUB = PIECE // 2
F32, BF16 = jnp.float32, jnp.bfloat16


def paley_table():
    members = [(a, b) for a in range(5) for b in range(5)]
    squares = set()
    for a, b in members:
        if (a, b) != (0, 0):
            squares.add(((a * a + 2 * b * b) % 5, 2 * a * b % 5))
    jacobsthal = np.zeros((25, 25))
    for i, (a, b) in enumerate(members):
        for j, (c, d) in enumerate(members):
            difference = ((a - c) % 5, (b - d) % 5)
            if difference != (0, 0):
                jacobsthal[i, j] = 1.0 if difference in squares else -1.0
    conference = np.zeros((26, 26))
    conference[0, 1:] = 1.0
    conference[1:, 0] = 1.0
    conference[1:, 1:] = jacobsthal
    hadamard = np.kron(conference, np.array([[1.0, -1.0], [-1.0, -1.0]]))
    return hadamard + np.kron(np.eye(26), np.array([[1.0, 1.0], [1.0, -1.0]]))


def sylvester(count):
    table = np.ones((1, 1))
    while table.shape[0] < count:
        table = np.kron(np.array([[1.0, 1.0], [1.0, -1.0]]), table)
    return table


def kernel(
    exponents_hbm, hidden_hbm, wide_hbm, weights_hbm, scale_hbm, residual_hbm, out_hbm,
    exponents, hidden, wide, weights, scale, residual,
    stage, got, stage_back, got_back, codes, sums,
    arrived_1, arrived_2, arrived_3,
    load_sem, out_send, out_recv, back_send, back_recv, own_sem,
    y_send, y_recv, pair_send, pair_recv, rs_send, rs_recv, out, write_sem,
):
    d, t = lax.axis_index("dp"), lax.axis_index("tensor")
    z, x = lax.div(t, RING), lax.rem(t, RING)
    core = lax.rem(d, 2)

    def loads():
        pairs = [
            (hidden_hbm, hidden), (wide_hbm, wide), (weights_hbm, weights),
            (scale_hbm, scale), (residual_hbm, residual), (exponents_hbm, exponents),
        ]
        return [pltpu.make_async_copy(src, dst, load_sem.at[i]) for i, (src, dst) in enumerate(pairs)]

    def dp_device(distance):
        return (lax.rem(d + 2 * distance + DP, DP), t)

    def pair_device():
        return (d + 1 - 2 * core, t)

    def plane_device(dz, dx):
        return (d, lax.rem(z + dz + RING, RING) * RING + lax.rem(x + dx + RING, RING))

    def offset_device(off):
        return plane_device(lax.div(off, RING), lax.rem(off, RING))

    def offset_source(off):
        return plane_device(-lax.div(off, RING), -lax.rem(off, RING))

    barrier = pltpu.get_barrier_semaphore()

    far_first = sorted(range(1, TENSOR), key=lambda off: -(min(off // RING, RING - off // RING) + min(off % RING, RING - off % RING)))
    for device in [plane_device(off // RING, off % RING) for off in far_first] + [dp_device(1), dp_device(-1), pair_device()]:
        pl.semaphore_signal(barrier, inc=1, device_id=device, device_id_type=pl.DeviceIdType.MESH)
    for load in loads():
        load.start()

    def remote(src, dst, send, recv, device):
        return pltpu.make_async_remote_copy(
            src_ref=src, dst_ref=dst, send_sem=send, recv_sem=recv,
            device_id=device, device_id_type=pl.DeviceIdType.MESH,
        )

    def holder(chunk, side, i):
        return RING * (chunk % 2 * 2 + side) + 2 * i + (side + chunk // 2) % 2

    odd = lax.rem(z + x, 2)
    first_row = lax.rem(z, 2) * 64 + (2 * odd + lax.div(z, 2)) * 16 + lax.div(x, 2) * 8

    def split(chunk):
        for side in range(2):
            block = hidden[side * 64 + chunk * 16 : side * 64 + chunk * 16 + 16, :].astype(F32)
            for i in range(2):
                rows = block[8 * i : 8 * i + 8]
                stage[holder(chunk, side, i)] = jnp.concatenate([rows[:, :WIDE], rows[:, WIDE:]], axis=0).astype(BF16)

    def out_copy(off):
        device = offset_device(off)
        return remote(stage.at[device[1]], got.at[t], out_send.at[off], out_recv.at[off], device)

    def out_begin(parity):
        turn = lax.rem(odd + parity, 2)

        def begin(i, carry):
            dz = lax.div(i, 2)
            out_copy(RING * dz + 2 * lax.rem(i, 2) + lax.rem(dz + turn, 2)).start()
            return carry

        lax.fori_loop(1 - turn, 8, begin, 0)

    loads()[0].wait()
    split(0)
    split(1)
    pl.semaphore_wait(barrier, TENSOR - 1 + 3)
    out_begin(0)
    split(2)
    split(3)
    out_begin(1)
    mine = pltpu.make_async_copy(stage.at[t], got.at[t], own_sem.at[0])
    mine.start()
    mine.wait()

    def out_wait(off, carry):
        sender = offset_source(off)[1]
        remote(stage.at[t], got.at[sender], out_send.at[off], out_recv.at[off], offset_device(off)).wait_recv()
        return carry

    lax.fori_loop(1, TENSOR, out_wait, 0)
    loads()[1].wait()
    loads()[5].wait()

    row = lax.broadcasted_iota(jnp.int32, (8, 1), 0)
    exponent = jnp.zeros((8, 1), jnp.int32)
    for r in range(8):
        exponent = jnp.where(row == r, exponents[first_row + r], exponent)
    power = jnp.left_shift(1, exponent + 3).astype(F32) * 0.125
    low, high = power * -8.0, power * 7.0

    def transform(at, size):
        left = got[...].reshape(TENSOR * 16, WIDE)
        product = jnp.dot(left, wide[:, pl.ds(at, size)], preferred_element_type=F32)
        parts = [product[8 * i : 8 * i + 8] for i in range(2 * TENSOR)]
        step = 1
        while step < len(parts):
            for i in range(len(parts)):
                if i & step == 0:
                    u, v = parts[i], parts[i + step]
                    parts[i], parts[i + step] = u + v, u - v
            step *= 2
        parts = [jnp.minimum(jnp.maximum(p * (1.0 / math.sqrt(FF)), low), high) for p in parts]
        for i in range(TENSOR):
            stage_back[i, :, pl.ds(at, size)] = jnp.concatenate(parts[2 * i : 2 * i + 2], axis=0).astype(BF16)

    spans = ((0, 768), (768, WIDE - 768))

    def back_copy(piece, off):
        device = offset_device(off)
        lanes = pl.ds(*spans[piece])
        return remote(
            stage_back.at[device[1], :, lanes], got_back.at[t, :, lanes],
            back_send.at[piece, off], back_recv.at[piece, off], device,
        )

    for piece in range(2):
        begin, size = spans[piece]

        def transform_step(i, carry):
            transform(pl.multiple_of(begin + i * 256, 256), 256)
            return carry

        lax.fori_loop(0, size // 256, transform_step, 0)
        if size % 256:
            transform(begin + size // 256 * 256, size % 256)

        def back_begin(off, carry):
            back_copy(piece, off).start()
            return carry

        lax.fori_loop(1, TENSOR, back_begin, 0)
        lanes = pl.ds(begin, size)
        pltpu.make_async_copy(stage_back.at[t, :, lanes], got_back.at[t, :, lanes], own_sem.at[1 + piece]).start()

    for piece in range(2):
        lanes = pl.ds(*spans[piece])
        pltpu.make_async_copy(stage_back.at[t, :, lanes], got_back.at[t, :, lanes], own_sem.at[1 + piece]).wait()

    def back_wait(sender):
        off = lax.rem(z - sender // RING + RING, RING) * RING + lax.rem(x - sender % RING + RING, RING)

        @pl.when(off > 0)
        def _():
            for piece in range(2):
                lanes = pl.ds(*spans[piece])
                remote(
                    stage_back.at[t, :, lanes], got_back.at[sender, :, lanes],
                    back_send.at[piece, off], back_recv.at[piece, off], offset_device(off),
                ).wait_recv()

    def collect(chunk):
        for side in range(2):
            senders = [holder(chunk, side, i) for i in range(2)]
            for sender in senders:
                back_wait(sender)
            blocks = [got_back[sender].astype(F32) for sender in senders]
            for half in range(2):
                rows = jnp.concatenate([b[8 * half : 8 * half + 8] for b in blocks], axis=0)
                codes[chunk, d, side * SUB : side * SUB + SUB, half * WIDE : half * WIDE + WIDE] = rows.astype(BF16)
        pair_copy(chunk, 0, False).start()

    def index(distance):
        return lax.rem(d + 2 * distance + DP, DP)

    def whole(chunk, distance):
        return codes.at[chunk, index(distance)]

    def part(chunk, distance, side):
        return codes.at[chunk, index(distance), side * SUB : side * SUB + SUB]

    def y_copy(chunk, kind, receiving):
        sign = -1 if kind % 2 else 1
        distance = -sign if kind in (2, 3) else 0
        ref = part(chunk, distance - sign if receiving else distance, kind % 2 if kind < 4 else 5 - kind)
        return remote(ref, ref, y_send.at[chunk, kind], y_recv.at[chunk, kind], dp_device(sign))

    def pair_copy(chunk, kind, receiving):
        def ref_of(base):
            if kind < 3:
                return codes.at[chunk, lax.rem(base + 2 * (0, -1, 1)[kind] + DP, DP)]
            return codes.at[chunk, lax.rem(base + 4, DP), (kind - 3) * SUB : (kind - 3) * SUB + SUB]

        ref = ref_of(pair_device()[0] if receiving else d)
        return remote(ref, ref, pair_send.at[chunk, kind], pair_recv.at[chunk, kind], pair_device())

    def send_own(chunk):
        for kind in (0, 1, 4, 5):
            y_copy(chunk, kind, False).start()

    def z_first(path):
        return path < PATHS // 2

    lanes = [slice(path * PART, path * PART + PART) for path in range(PATHS)]
    bufs = (arrived_1, arrived_2, arrived_3)

    def group(chunk, path, target, side=None):
        return (chunk, path, target, slice(None) if side is None else slice(2 * side, 2 * side + 2))

    def block(chunk, path, target):
        return (chunk, path, z if z_first(path) else x, target)

    def axes(path, phase):
        along_z = z_first(path) == (phase == 0)
        if along_z:
            return z, lambda n: plane_device(n, 0)
        return x, lambda n: plane_device(0, n)

    def rs_copy(chunk, path, step, way):
        sign = (1, -1, 2)[way]
        here, device = axes(path, step // 2)
        target = lax.rem(here + (2 if step == 0 else sign) + RING, RING)
        if step == 0:
            src = sums.at[group(chunk, path, target, way)]
        elif step == 1:
            src = sums.at[group(chunk, path, target)]
        else:
            src = sums.at[block(chunk, path, target)]
        number = path * 7 + step * 2 + way
        return remote(
            src, bufs[step].at[chunk, path, way],
            rs_send.at[chunk, number], rs_recv.at[chunk, number], device(sign),
        )

    def rs_start(chunk, path, step):
        for way in range(3 if step == 2 else 2):
            rs_copy(chunk, path, step, way).start()

    def rs_second(chunk, path):
        here, _ = axes(path, 0)
        for way in range(2):
            rs_copy(chunk, path, 0, way).wait_recv()
            where = group(chunk, path, lax.rem(here + (1, -1)[way] + RING, RING), way)
            sums[where] = (sums[where].astype(F32) + bufs[0][chunk, path, way].astype(F32)).astype(BF16)
            rs_copy(chunk, path, 1, way).start()

    def rs_third(chunk, path):
        where = group(chunk, path, axes(path, 0)[0])
        total = sums[where].astype(F32)
        for way in range(2):
            rs_copy(chunk, path, 1, way).wait_recv()
            total += bufs[1][chunk, path, way].astype(F32)
        sums[where] = total.astype(BF16)
        rs_start(chunk, path, 2)

    def write(chunk, path):
        where = (slice(chunk * SUB, chunk * SUB + SUB), lanes[path])
        return pltpu.make_async_copy(out.at[where], out_hbm.at[where], write_sem.at[chunk, path])

    def rs_finish(chunk, path):
        total = sums[block(chunk, path, axes(path, 1)[0])].astype(F32)
        for way in range(3):
            rs_copy(chunk, path, 2, way).wait_recv()
            total += bufs[2][chunk, path, way].astype(F32)
        rows, cols = slice(chunk * SUB, chunk * SUB + SUB), lanes[path]
        out[rows, cols] = (total * scale[:, cols] + residual[rows, cols].astype(F32)).astype(BF16)
        write(chunk, path).start()

    height = lax.div(d, 2)

    def multiply_own(path):
        def tile(i, carry):
            at = pl.multiple_of(i * 512, 512)
            left = codes[:, pl.ds(2 * height, 2)].reshape(CHUNKS * 2 * PIECE, WIDTH)
            product = jnp.dot(left, weights[:, pl.ds(path * PART + at, 512)], preferred_element_type=F32)
            rows = product.astype(BF16).reshape(CHUNKS, RING, SUB, 512)
            if z_first(path):
                sums[:, path, height, :, :, pl.ds(at, 512)] = rows
            else:
                sums[:, path, :, height, :, pl.ds(at, 512)] = rows
            return carry

        lax.fori_loop(0, PART // 512, tile, 0)

    def multiply(chunk, path):
        width = PART if chunk == CHUNKS - 1 else 512
        others = [lax.rem(height + i, RING) for i in range(1, RING)]

        def tile(i, carry):
            at = pl.multiple_of(i * width, width)
            left = jnp.concatenate([codes[chunk, pl.ds(2 * o, 2)].reshape(2 * PIECE, WIDTH) for o in others], axis=0)
            product = jnp.dot(left, weights[:, pl.ds(path * PART + at, width)], preferred_element_type=F32).astype(BF16)
            for j, o in enumerate(others):
                rows = product[j * 2 * PIECE : (j + 1) * 2 * PIECE].reshape(RING, SUB, width)
                if z_first(path):
                    sums[chunk, path, o, :, :, pl.ds(at, width)] = rows
                else:
                    sums[chunk, path, :, o, :, pl.ds(at, width)] = rows
            return carry

        lax.fori_loop(0, PART // width, tile, 0)

    def near(chunk):
        for kind in range(2):
            y_copy(chunk, kind, True).wait_recv()
            y_copy(chunk, kind + 2, False).start()

    def rest(chunk):
        for kind in range(2):
            y_copy(chunk, kind + 4, True).wait_recv()
            pair_copy(chunk, kind + 1, False).start()

    def far(chunk):
        for kind in range(2):
            y_copy(chunk, kind + 2, True).wait_recv()
            pair_copy(chunk, kind + 3, False).start()

    def own(path):
        if path == 0:
            for i in (2, 3, 4):
                loads()[i].wait()
            for chunk in range(CHUNKS):
                pair_copy(chunk, 0, True).wait_recv()
        multiply_own(path)

    def product(chunk, path):
        if path == 0:
            for kind in range(1, 5):
                pair_copy(chunk, kind, True).wait_recv()
        multiply(chunk, path)
        rs_start(chunk, path, 0)

    def reduce(chunk, path, step):
        (rs_second, rs_third, None, rs_finish)[step - 2](chunk, path)

    def drain(off, carry):
        out_copy(off).wait_send()
        for piece in range(2):
            back_copy(piece, off).wait_send()
        return carry

    def sent(chunk):
        for kind in range(6):
            y_copy(chunk, kind, False).wait_send()
        for kind in range(5):
            pair_copy(chunk, kind, False).wait_send()

    def passed(chunk, steps):
        for path in range(PATHS):
            for step in steps:
                for way in range(3 if step == 2 else 2):
                    rs_copy(chunk, path, step, way).wait_send()

    collect(0)
    send_own(0)
    collect(1)
    collect(2)
    collect(3)
    near(0)
    lax.fori_loop(1, TENSOR, drain, 0)
    own(0)
    send_own(1)
    own(1)
    rest(0)
    far(0)
    near(1)
    send_own(2)
    product(0, 0)
    product(0, 1)
    rest(1)
    far(1)
    reduce(0, 0, 2)
    near(2)
    send_own(3)
    reduce(0, 1, 2)
    product(1, 0)
    rest(2)
    product(1, 1)
    far(2)
    reduce(1, 0, 2)
    near(3)
    reduce(0, 0, 3)
    reduce(0, 1, 3)
    product(2, 0)
    reduce(1, 1, 2)
    rest(3)
    product(2, 1)
    far(3)
    reduce(1, 0, 3)
    product(3, 0)
    product(3, 1)
    reduce(2, 0, 2)
    reduce(2, 1, 2)
    reduce(3, 0, 2)
    reduce(0, 0, 5)
    reduce(3, 1, 2)
    reduce(2, 0, 3)
    reduce(1, 1, 3)
    reduce(1, 0, 5)
    reduce(2, 1, 3)
    reduce(3, 0, 3)
    reduce(3, 1, 3)
    reduce(1, 1, 5)
    reduce(0, 1, 5)
    reduce(2, 1, 5)
    reduce(2, 0, 5)
    reduce(3, 0, 5)
    reduce(3, 1, 5)
    for chunk in range(CHUNKS):
        sent(chunk)
        passed(chunk, (0, 1, 2))
        for path in range(PATHS):
            write(chunk, path).wait()


def shards(hidden, exponents, weight_levels, column_scale, residual):
    wide = np.kron(sylvester(32), paley_table()).astype(ml_dtypes.bfloat16)
    anywhere = pl.BlockSpec(memory_space=pl.ANY)
    dma = pltpu.SemaphoreType.DMA

    def vmem(*shape, dtype=BF16):
        return pltpu.VMEM(shape, dtype)

    return pl.pallas_call(
        kernel,
        out_shape=jax.ShapeDtypeStruct(residual.shape, BF16),
        in_specs=[anywhere] * 6,
        out_specs=anywhere,
        scratch_shapes=[
            pltpu.SMEM((ROWS,), jnp.int32), vmem(ROWS, WIDTH), vmem(WIDE, WIDE), vmem(WIDTH, COLS), vmem(1, COLS, dtype=F32), vmem(ROWS // 2, COLS),
            *[vmem(TENSOR, 16, WIDE) for _ in range(4)],
            vmem(CHUNKS, DP, PIECE, WIDTH), vmem(CHUNKS, PATHS, RING, RING, SUB, PART),
            *[
                vmem(CHUNKS, PATHS, *shape)
                for shape in ((2, 2, SUB, PART), (2, RING, SUB, PART), (3, SUB, PART))
            ],
            dma((6,)), dma((TENSOR,)), dma((TENSOR,)), dma((2, TENSOR)), dma((2, TENSOR)), dma((3,)),
            dma((CHUNKS, 6)), dma((CHUNKS, 6)), dma((CHUNKS, 5)), dma((CHUNKS, 5)),
            dma((CHUNKS, 7 * PATHS)), dma((CHUNKS, 7 * PATHS)),
            vmem(ROWS // 2, COLS), dma((CHUNKS, PATHS)),
        ],
        compiler_params=pltpu.CompilerParams(
            collective_id=0, has_side_effects=True, vmem_limit_bytes=60 * 1024 * 1024,
        ),
        cost_estimate=pl.CostEstimate(flops=15_400_000_000, bytes_accessed=21_000_000, transcendentals=0),
    )(exponents, hidden, wide, weight_levels, column_scale.reshape(1, COLS), residual)


def solution(mesh):
    return jax.shard_map(
        shards,
        mesh=mesh,
        in_specs=(P("dp", "tensor"), P("dp"), P("tensor", "dp"), P("dp"), P("tensor", "dp")),
        out_specs=P("tensor", "dp"),
        check_vma=False,
    )
```
